32 devices in a mesh: wide: 8 (over z, y), narrow: 4 (over x, core).
Axes of the slice: x: 2, y: 2, z: 4, core: 2. Of those that a mesh axis runs over, the one named last changes fastest.
Arguments:
- quantized_inputs: bfloat16 [16384, 3072], P(('wide', 'narrow')), may hold values from -6 to 6
- x_full: bfloat16 [16384, 3072], P(('wide', 'narrow')), may hold values from -6 to 6
Outputs:
- gram_out: float32 [8, 4, 512, 16384], P(None, 'narrow', None, 'wide')
- cross_gram_result: float32 [8, 4, 512, 16384], P(None, 'narrow', None, 'wide')
The draws below stay inside these ranges and needn't reach their ends.
All inputs are finite; a program needn't handle non-finite values.
Results may differ from the reference program's by a relative error of at most 0.003.
Values may be sent and summed in bfloat16 or wider, within the bound.
No kernel may reach another device: no remote copies, remote signals or barrier semaphores. Data moves between devices by JAX's collectives and lax.ppermute only.
A program may use at most 256 MiB of HBM per device.

```python
import jax
import jax.numpy as jnp

D = 16384
TOKENS = 3072
WIDE_DEVS = 8
NARROW_DEVS = 4
FD = 512


def block_scale(own_key, shape, shards, smallest, top_value):
    level = 1.0
    for axis_at, shards_of in shards:
        heights = jax.random.uniform(jax.random.fold_in(jax.random.fold_in(own_key, 6), axis_at), (shards_of,), jnp.float32, smallest / len(shards), top_value / len(shards))
        level = level * jnp.repeat(jnp.exp(heights), shape[axis_at] // shards_of).reshape((-1,) + (1,) * (len(shape) - 1 - axis_at))
    return level


def scatter_about(own_key, extent, deviation, bound, shards=(), dtype=jnp.bfloat16):
    result = jax.random.normal(own_key, extent, jnp.float32) * deviation
    if len(shards) > 0:
        result = block_scale(own_key, extent, shards, -0.22, 0.18) * result
    return jnp.clip(result, min=-bound, max=bound).astype(dtype)


def setup_inputs(seed: int = 0) -> dict:
    keys = jax.random.split(jax.random.key(seed), 3)
    return {
        "quantized_inputs": scatter_about(keys[0], (D, TOKENS), 1.0, 6.0, ((0, 32),)),
        "x_full": scatter_about(keys[1], (D, TOKENS), 1.0, 6.0, ((0, 32),)),
    }


def reference(quantized_inputs, x_full):
    difference = (x_full.astype(jnp.float32) - quantized_inputs.astype(jnp.float32)).astype(jnp.bfloat16)
    complete_gram = jnp.dot(quantized_inputs, quantized_inputs.T, preferred_element_type=jnp.float32) / TOKENS
    cross_whole = jnp.dot(difference, quantized_inputs.T, preferred_element_type=jnp.float32) / TOKENS
    gram_out = complete_gram.reshape(WIDE_DEVS, NARROW_DEVS, FD, D)
    cross_gram_result = cross_whole.reshape(WIDE_DEVS, NARROW_DEVS, FD, D)
    return gram_out, cross_gram_result
```

```python
import jax
import jax.numpy as jnp
from jax import lax
from jax.sharding import PartitionSpec as P


def ring_order(count):
    return [i for i in range(0, count, 2)] + [i for i in reversed(range(1, count, 2))]


def per_device(quantized_inputs, x_full):
    token_count = quantized_inputs.shape[1]
    owned_rows = quantized_inputs.shape[0]
    wide_count = lax.axis_size("wide")
    order = ring_order(wide_count)
    forward = [(order[i], order[(i + 1) % wide_count]) for i in range(wide_count)]
    backward = [(b, a) for a, b in forward]
    place = [0] * wide_count
    for i, w in enumerate(order):
        place[w] = i
    me = jnp.asarray(place, jnp.int32)[lax.axis_index("wide")]
    order_table = jnp.asarray(order, jnp.int32)

    difference = (x_full.astype(jnp.float32) - quantized_inputs.astype(jnp.float32)).astype(
        jnp.bfloat16
    )
    right = lax.all_gather(quantized_inputs, "narrow", axis=0, tiled=True)
    columns = right.shape[0]

    far, near = wide_count // 2, (wide_count - 1) // 2
    quantized_at = {0: quantized_inputs}
    difference_at = {0: difference}
    fq, fd, bq, bd = quantized_inputs, difference, quantized_inputs, difference
    for step in range(1, far + 1):
        fq = lax.ppermute(fq, "wide", forward)
        quantized_at[step] = fq
        bd = lax.ppermute(bd, "wide", backward)
        difference_at[wide_count - step] = bd
        if step <= near:
            bq = lax.ppermute(bq, "wide", backward)
            quantized_at[wide_count - step] = bq
            fd = lax.ppermute(fd, "wide", forward)
            difference_at[step] = fd

    gram_out = jnp.zeros((wide_count, 1, owned_rows, columns), jnp.float32)
    cross_gram_result = jnp.zeros((wide_count, 1, owned_rows, columns), jnp.float32)

    def statistic(left):
        product = jnp.einsum("ia,ea->ie", left, right, preferred_element_type=jnp.float32)
        return (product / token_count)[None, None]

    offsets = [0]
    for step in range(1, far + 1):
        offsets += [step] if wide_count - step == step else [step, wide_count - step]
    for offset in offsets:
        owner = order_table[(me - offset + wide_count) % wide_count]
        gram_out = lax.dynamic_update_slice(
            gram_out, statistic(quantized_at[offset]), (owner, 0, 0, 0)
        )
        cross_gram_result = lax.dynamic_update_slice(
            cross_gram_result, statistic(difference_at[offset]), (owner, 0, 0, 0)
        )
    return (gram_out, cross_gram_result)


def solution(mesh):
    return jax.shard_map(
        per_device,
        mesh=mesh,
        in_specs=(P(("wide", "narrow"), None), P(("wide", "narrow"), None)),
        out_specs=(P(None, "narrow", None, "wide"), P(None, "narrow", None, "wide")),
        check_vma=False,
    )
```

```python
import functools

import jax
import jax.numpy as jnp
from jax import lax
from jax.experimental import pallas as pl
from jax.experimental.pallas import tpu as pltpu
from jax.sharding import PartitionSpec as P

TILE = 512


def product_kernel(scale, place_ref, left_ref, right_ref, *refs):
    total = lax.dot_general(
        left_ref[...],
        right_ref[...],
        (((1,), (1,)), ((), ())),
        preferred_element_type=jnp.float32,
    )
    result_ref = refs[-1]
    result_ref[...] = (total * scale).astype(result_ref.dtype).reshape(result_ref.shape)


def product(left, right, owner=None, out=None, out_shape=None):
    rows, tokens = left.shape
    columns = right.shape[0]
    tile = min(TILE, columns)
    if owner is None:
        owner = 0
        out_spec = pl.BlockSpec((rows, tile), lambda j, at: (0, j))
        shape = jax.ShapeDtypeStruct((rows, columns), jnp.bfloat16)
    else:
        out_spec = pl.BlockSpec((1, 1, rows, tile), lambda j, at: (at[0], 0, 0, j))
        shape = jax.ShapeDtypeStruct(out_shape, jnp.float32)
    in_specs = [
        pl.BlockSpec((rows, tokens), lambda j, at: (0, 0)),
        pl.BlockSpec((tile, tokens), lambda j, at: (j, 0)),
    ]
    operands = [jnp.asarray(owner, jnp.int32).reshape(1), left, right]
    aliases = {}
    if out is not None:
        aliases = {len(operands): 0}
        in_specs.append(pl.BlockSpec(memory_space=pl.ANY))
        operands.append(out)
    return pl.pallas_call(
        functools.partial(product_kernel, 1.0 / tokens),
        out_shape=shape,
        grid_spec=pltpu.PrefetchScalarGridSpec(
            num_scalar_prefetch=1,
            grid=(columns // tile,),
            in_specs=in_specs,
            out_specs=out_spec,
        ),
        input_output_aliases=aliases,
        compiler_params=pltpu.CompilerParams(vmem_limit_bytes=32 * 1024 * 1024),
        cost_estimate=pl.CostEstimate(
            flops=2 * rows * columns * tokens,
            bytes_accessed=2 * (rows + columns) * tokens + 4 * rows * columns,
            transcendentals=0,
        ),
    )(*operands)


def ring_order(count):
    return [i for i in range(0, count, 2)] + [i for i in reversed(range(1, count, 2))]


def per_device(quantized_inputs, x_full):
    owned_rows = quantized_inputs.shape[0]
    wide_count = lax.axis_size("wide")
    columns = owned_rows * lax.axis_size("narrow")
    order = ring_order(wide_count)
    forward = [(order[i], order[(i + 1) % wide_count]) for i in range(wide_count)]
    pairs = (forward, [(b, a) for a, b in forward])
    place = [order.index(w) for w in range(wide_count)]
    me = jnp.asarray(place, jnp.int32)[lax.axis_index("wide")]

    def owner_of(way, distance):
        offset = distance if way == 1 else -distance
        return jnp.asarray(order, jnp.int32)[(me + offset + wide_count) % wide_count]

    out_shape = (wide_count, 1, owned_rows, columns)
    outs = [None, None]
    now = []

    def tie(value):
        held = [i for i in range(2) if outs[i] is not None]
        done = lax.optimization_barrier((value, *[outs[i] for i in held], *now))
        for place_of, i in enumerate(held):
            outs[i] = done[1 + place_of]
        return done[0]

    def put(which, owner, block):
        outs[which] = product(tie(block), right_own, owner, outs[which], out_shape)

    def put_arrived(which, owner, block):
        outs[which] = lax.dynamic_update_slice(
            outs[which], tie(block).astype(jnp.float32)[None, None], (owner, 0, 0, 0)
        )

    def gather(block):
        return lax.all_gather(block, "narrow", axis=0, tiled=True)

    q = quantized_inputs
    d = (x_full.astype(jnp.float32) - q.astype(jnp.float32)).astype(jnp.bfloat16)
    right_own = gather(q)

    far, near = wide_count // 2, (wide_count - 1) // 2
    reach = {(0, 0): far, (0, 1): near, (1, 0): near, (1, 1): far}
    raw = {chain: max(hops - 1, min(hops, 1)) for chain, hops in reach.items()}
    at = {(which, way): [(q, d)[which]] for which in range(2) for way in range(2)}

    def start(which, step):
        for way in range(2):
            chain = (which, way)
            if step <= raw[chain]:
                block = at[chain][step - 1]
                block = block if step == 1 else tie(block)
                at[chain].append(lax.ppermute(block, "wide", pairs[way]))

    def arrivals(which, step):
        return [at[which, way][step] for way in range(2) if step <= raw[which, way]]

    start(0, 1)
    start(1, 1)
    right_next = [None, None]
    results = []
    for step in range(1, far + 1):
        if arrivals(0, step):
            now[:] = arrivals(0, step)
            start(0, step + 1)
            if step == 1:
                for way in range(2):
                    if raw[0, 1 - way] >= 1:
                        right_next[way] = gather(tie(at[0, 1 - way][1]))
        if arrivals(1, step):
            now[:] = arrivals(1, step)
            start(1, step + 1)
        sent = []
        for which in (1, 0):
            for way in range(2):
                if step == raw[which, way] < reach[which, way]:
                    result = product(tie(at[which, way][step]), right_next[way])
                    sent.append(result)
                    results.append(
                        (which, owner_of(way, step + 1), lax.ppermute(result, "wide", pairs[way]))
                    )
        now += sent
        if step == 1:
            put(0, lax.axis_index("wide"), q)
            put(1, lax.axis_index("wide"), d)
        for which in range(2):
            for way in range(2):
                if step <= raw[which, way]:
                    put(which, owner_of(way, step), at[which, way][step])
    now[:] = []
    for result in results:
        put_arrived(*result)
    return tuple(outs)


def solution(mesh):
    return jax.shard_map(
        per_device,
        mesh=mesh,
        in_specs=(P(("wide", "narrow"), None), P(("wide", "narrow"), None)),
        out_specs=(P(None, "narrow", None, "wide"), P(None, "narrow", None, "wide")),
        check_vma=False,
    )
```

```python
import functools

import jax
import jax.numpy as jnp
from jax import lax
from jax.experimental import pallas as pl
from jax.experimental.pallas import tpu as pltpu
from jax.sharding import PartitionSpec as P

TILE = 512
LAST_PIECES = 2


def product_kernel(scale, place_ref, left_ref, right_ref, *refs):
    total = lax.dot_general(
        left_ref[...],
        right_ref[...],
        (((1,), (1,)), ((), ())),
        preferred_element_type=jnp.float32,
    )
    result_ref = refs[-1]
    result_ref[...] = (total * scale).astype(result_ref.dtype).reshape(result_ref.shape)


def product(left, right, owner=None, out=None, out_shape=None, piece=0, pieces=1):
    rows, tokens = left.shape[0] // pieces, left.shape[1]
    columns = right.shape[0]
    tile = min(TILE, columns)
    if owner is None:
        owner = 0
        out_spec = pl.BlockSpec((rows, tile), lambda j, at: (0, j))
        shape = jax.ShapeDtypeStruct((rows, columns), jnp.bfloat16)
    else:
        out_spec = pl.BlockSpec((1, 1, rows, tile), lambda j, at: (at[0], 0, 0, j))
        shape = jax.ShapeDtypeStruct(out_shape, jnp.float32)
    in_specs = [
        pl.BlockSpec((rows, tokens), lambda j, at: (piece, 0)),
        pl.BlockSpec((tile, tokens), lambda j, at: (j, 0)),
    ]
    operands = [jnp.asarray(owner, jnp.int32).reshape(1), left, right]
    aliases = {}
    if out is not None:
        aliases = {len(operands): 0}
        in_specs.append(pl.BlockSpec(memory_space=pl.ANY))
        operands.append(out)
    return pl.pallas_call(
        functools.partial(product_kernel, 1.0 / tokens),
        out_shape=shape,
        grid_spec=pltpu.PrefetchScalarGridSpec(
            num_scalar_prefetch=1,
            grid=(columns // tile,),
            in_specs=in_specs,
            out_specs=out_spec,
        ),
        input_output_aliases=aliases,
        compiler_params=pltpu.CompilerParams(vmem_limit_bytes=32 * 1024 * 1024),
        cost_estimate=pl.CostEstimate(flops=0, bytes_accessed=0, transcendentals=0),
    )(*operands)


def ring_order(count):
    return [i for i in range(0, count, 2)] + [i for i in reversed(range(1, count, 2))]


def per_device(quantized_inputs, x_full):
    owned_rows = quantized_inputs.shape[0]
    wide_count = lax.axis_size("wide")
    columns = owned_rows * lax.axis_size("narrow")
    order = ring_order(wide_count)
    forward = [(order[i], order[(i + 1) % wide_count]) for i in range(wide_count)]
    pairs = (forward, [(b, a) for a, b in forward])
    place = [order.index(w) for w in range(wide_count)]
    me = jnp.asarray(place, jnp.int32)[lax.axis_index("wide")]

    def owner_of(way, distance):
        offset = distance if way == 1 else -distance
        return jnp.asarray(order, jnp.int32)[(me + offset + wide_count) % wide_count]

    out_shape = (wide_count, 1, owned_rows, columns)
    outs = [None, None]
    now = []

    def tie(value, *others):
        held = [i for i in range(2) if outs[i] is not None]
        done = lax.optimization_barrier((value, *[outs[i] for i in held], *now, *others))
        for place_of, i in enumerate(held):
            outs[i] = done[1 + place_of]
        return done[0]

    def put(which, owner, block):
        outs[which] = product(tie(block), right_own, owner, outs[which], out_shape)

    def put_arrived(which, owner, block, first_row):
        outs[which] = lax.dynamic_update_slice(
            outs[which], block.astype(jnp.float32)[None, None], (owner, 0, first_row, 0)
        )

    def gather(block, *others):
        return lax.all_gather(tie(block, *others), "narrow", axis=0, tiled=True)

    q = quantized_inputs
    d = (x_full.astype(jnp.float32) - q.astype(jnp.float32)).astype(jnp.bfloat16)
    right_own = gather(q)

    far, near = wide_count // 2, (wide_count - 1) // 2
    reach = {(0, 0): far, (0, 1): near, (1, 0): near, (1, 1): far}
    raw = {chain: max(hops - 1, min(hops, 1)) for chain, hops in reach.items()}
    at = {(which, way): [(q, d)[which]] for which in range(2) for way in range(2)}

    def start(which, step):
        for way in range(2):
            chain = (which, way)
            if step <= raw[chain]:
                block = at[chain][step - 1]
                block = block if step == 1 else tie(block)
                at[chain].append(lax.ppermute(block, "wide", pairs[way]))

    def arrivals(which, step):
        return [at[which, way][step] for way in range(2) if step <= raw[which, way]]

    start(0, 1)
    start(1, 1)
    right_next = [None, None]
    results = []
    for step in range(1, far + 1):
        for which in range(2):
            if not arrivals(which, step):
                continue
            now[:] = arrivals(which, step)
            start(which, step + 1)
            if step == 1 and which == 0:
                for way in range(2):
                    if raw[0, 1 - way] >= 1:
                        right_next[way] = gather(at[0, 1 - way][1], d)
            together = step in (1, far - 1)
            if which == 0 and together:
                continue
            if which == 1:
                for sent, way in ((1, 0), (0, 1), (1, 1), (0, 0)):
                    if step == raw[sent, way] < reach[sent, way]:
                        pieces = LAST_PIECES if step == far - 1 else 1
                        for i in range(pieces):
                            result = product(
                                tie(at[sent, way][step]), right_next[way], piece=i, pieces=pieces
                            )
                            now.append(result)
                            results.append((
                                sent,
                                owner_of(way, step + 1),
                                lax.ppermute(result, "wide", pairs[way]),
                                i * owned_rows // pieces,
                            ))
            if step == 1:
                put(0, lax.axis_index("wide"), q)
                put(1, lax.axis_index("wide"), d)
            for own in range(2) if together else (which,):
                for way in range(2):
                    if step <= raw[own, way]:
                        put(own, owner_of(way, step), at[own, way][step])
    for result in sorted(results, key=lambda result: result[3]):
        put_arrived(*result)
    return tuple(outs)


def solution(mesh):
    return jax.shard_map(
        per_device,
        mesh=mesh,
        in_specs=(P(("wide", "narrow"), None), P(("wide", "narrow"), None)),
        out_specs=(P(None, "narrow", None, "wide"), P(None, "narrow", None, "wide")),
        check_vma=False,
    )
```

```python
import functools

import jax
import jax.numpy as jnp
from jax import lax
from jax.experimental import pallas as pl
from jax.experimental.pallas import tpu as pltpu
from jax.sharding import PartitionSpec as P

TILE = 512
QUARTERS = 4


def product_kernel(scale, place_ref, left_ref, right_ref, *refs):
    total = lax.dot_general(
        left_ref[...],
        right_ref[...],
        (((1,), (1,)), ((), ())),
        preferred_element_type=jnp.float32,
    )
    result_ref = refs[-1]
    result_ref[...] = (total * scale).astype(result_ref.dtype).reshape(result_ref.shape)


def product(left, right, owner=None, out=None, out_shape=None, first_row=0, rows=None):
    rows, tokens = rows or left.shape[0], left.shape[1]
    columns = right.shape[0]
    tile = min(TILE, columns)
    if owner is None:
        owner = 0
        out_spec = pl.BlockSpec((rows, tile), lambda j, at: (0, j))
        shape = jax.ShapeDtypeStruct((rows, columns), jnp.bfloat16)
    else:
        out_spec = pl.BlockSpec((1, 1, rows, tile), lambda j, at: (at[0], 0, 0, j))
        shape = jax.ShapeDtypeStruct(out_shape, jnp.float32)
    in_specs = [
        pl.BlockSpec((rows, tokens), lambda j, at: (first_row // rows, 0)),
        pl.BlockSpec((tile, tokens), lambda j, at: (j, 0)),
    ]
    operands = [jnp.asarray(owner, jnp.int32).reshape(1), left, right]
    aliases = {}
    if out is not None:
        aliases = {len(operands): 0}
        in_specs.append(pl.BlockSpec(memory_space=pl.ANY))
        operands.append(out)
    return pl.pallas_call(
        functools.partial(product_kernel, 1.0 / tokens),
        out_shape=shape,
        grid_spec=pltpu.PrefetchScalarGridSpec(
            num_scalar_prefetch=1,
            grid=(columns // tile,),
            in_specs=in_specs,
            out_specs=out_spec,
        ),
        input_output_aliases=aliases,
        compiler_params=pltpu.CompilerParams(vmem_limit_bytes=32 * 1024 * 1024),
        cost_estimate=pl.CostEstimate(flops=0, bytes_accessed=0, transcendentals=0),
    )(*operands)


def ring_order(count):
    return [i for i in range(0, count, 2)] + [i for i in reversed(range(1, count, 2))]


def per_device(quantized_inputs, x_full):
    owned_rows = quantized_inputs.shape[0]
    wide_count = lax.axis_size("wide")
    columns = owned_rows * lax.axis_size("narrow")
    order = ring_order(wide_count)
    forward = [(order[i], order[(i + 1) % wide_count]) for i in range(wide_count)]
    pairs = (forward, [(b, a) for a, b in forward])
    place = [order.index(w) for w in range(wide_count)]
    me = jnp.asarray(place, jnp.int32)[lax.axis_index("wide")]

    def owner_of(way, distance):
        offset = distance if way == 1 else -distance
        return jnp.asarray(order, jnp.int32)[(me + offset + wide_count) % wide_count]

    out_shape = (wide_count, 1, owned_rows, columns)
    outs = [None, None]
    now = []

    def tie(value, *others):
        held = [i for i in range(2) if outs[i] is not None]
        done = lax.optimization_barrier((value, *[outs[i] for i in held], *now, *others))
        for place_of, i in enumerate(held):
            outs[i] = done[1 + place_of]
        return done[0]

    def put(which, owner, block):
        outs[which] = product(tie(block), right_own, owner, outs[which], out_shape)

    def put_arrived(which, owner, block, first_row):
        outs[which] = lax.dynamic_update_slice(
            outs[which], tie(block).astype(jnp.float32)[None, None], (owner, 0, first_row, 0)
        )

    def gather(block, *others):
        return lax.all_gather(tie(block, *others), "narrow", axis=0, tiled=True)

    q = quantized_inputs
    d = (x_full.astype(jnp.float32) - q.astype(jnp.float32)).astype(jnp.bfloat16)
    right_own = gather(q)

    far, near = wide_count // 2, (wide_count - 1) // 2
    reach = {(0, 0): far, (0, 1): near, (1, 0): near, (1, 1): far}
    raw = {chain: max(hops - 1, min(hops, 1)) for chain, hops in reach.items()}
    at = {(which, way): [(q, d)[which]] for which in range(2) for way in range(2)}

    def start(which, step):
        for way in range(2):
            chain = (which, way)
            if step <= raw[chain]:
                block = at[chain][step - 1]
                block = block if step == 1 else tie(block)
                at[chain].append(lax.ppermute(block, "wide", pairs[way]))

    def arrivals(which, step):
        return [at[which, way][step] for way in range(2) if step <= raw[which, way]]

    start(0, 1)
    start(1, 1)
    right_next = [None, None]
    results = []
    for step in range(1, far + 1):
        for which in range(2):
            if not arrivals(which, step):
                continue
            now[:] = arrivals(which, step)
            start(which, step + 1)
            if step == 1 and which == 0:
                for way in range(2):
                    if raw[0, 1 - way] >= 1:
                        right_next[way] = gather(at[0, 1 - way][1], d)
            together = step in (1, far - 1)
            if which == 0 and together:
                continue
            if which == 1:
                for sent, way in ((1, 0), (0, 1), (1, 1), (0, 0)):
                    if step == raw[sent, way] < reach[sent, way]:
                        cut = owned_rows - owned_rows // QUARTERS if step == far - 1 else owned_rows
                        for first_row, rows in ((0, cut), (cut, owned_rows - cut)):
                            if rows == 0:
                                continue
                            result = product(
                                tie(at[sent, way][step]),
                                right_next[way],
                                first_row=first_row,
                                rows=rows,
                            )
                            now.append(result)
                            results.append((
                                sent,
                                owner_of(way, step + 1),
                                lax.ppermute(result, "wide", pairs[way]),
                                first_row,
                            ))
            if step == 1:
                put(0, lax.axis_index("wide"), q)
                put(1, lax.axis_index("wide"), d)
            for own in range(2) if together else (which,):
                for way in range(2):
                    if step <= raw[own, way]:
                        put(own, owner_of(way, step), at[own, way][step])
    now[:] = []
    for result in sorted(results, key=lambda result: result[3]):
        put_arrived(*result)
    return tuple(outs)


def solution(mesh):
    return jax.shard_map(
        per_device,
        mesh=mesh,
        in_specs=(P(("wide", "narrow"), None), P(("wide", "narrow"), None)),
        out_specs=(P(None, "narrow", None, "wide"), P(None, "narrow", None, "wide")),
        check_vma=False,
    )
```

```python
import functools

import jax
import jax.numpy as jnp
from jax import lax
from jax.experimental import pallas as pl
from jax.experimental.pallas import tpu as pltpu
from jax.sharding import PartitionSpec as P

TILE = 512
QUARTERS = 4


def product_kernel(scale, place_ref, left_ref, right_ref, *refs):
    total = lax.dot_general(
        left_ref[...],
        right_ref[...],
        (((1,), (1,)), ((), ())),
        preferred_element_type=jnp.float32,
    )
    result_ref = refs[-1]
    result_ref[...] = (total * scale).astype(result_ref.dtype).reshape(result_ref.shape)


def product(left, right, rows=None, row=0, owner=None, out=None, out_shape=None, out_row=0):
    rows, tokens = rows or left.shape[0], left.shape[1]
    columns = right.shape[0]
    tile = min(TILE, columns)
    if owner is None:
        owner = 0
        out_spec = pl.BlockSpec((rows, tile), lambda j, at: (0, j))
        shape = jax.ShapeDtypeStruct((rows, columns), jnp.bfloat16)
    else:
        out_spec = pl.BlockSpec((1, 1, rows, tile), lambda j, at: (at[0], 0, out_row // rows, j))
        shape = jax.ShapeDtypeStruct(out_shape, jnp.float32)
    in_specs = [
        pl.BlockSpec((rows, tokens), lambda j, at: (row // rows, 0)),
        pl.BlockSpec((tile, tokens), lambda j, at: (j, 0)),
    ]
    operands = [jnp.asarray(owner, jnp.int32).reshape(1), left, right]
    aliases = {}
    if out is not None:
        aliases = {len(operands): 0}
        in_specs.append(pl.BlockSpec(memory_space=pl.ANY))
        operands.append(out)
    return pl.pallas_call(
        functools.partial(product_kernel, 1.0 / tokens),
        out_shape=shape,
        grid_spec=pltpu.PrefetchScalarGridSpec(
            num_scalar_prefetch=1,
            grid=(columns // tile,),
            in_specs=in_specs,
            out_specs=out_spec,
        ),
        input_output_aliases=aliases,
        compiler_params=pltpu.CompilerParams(vmem_limit_bytes=48 * 1024 * 1024),
        cost_estimate=pl.CostEstimate(flops=0, bytes_accessed=0, transcendentals=0),
    )(*operands)


def ring_order(count):
    return [i for i in range(0, count, 2)] + [i for i in reversed(range(1, count, 2))]


def per_device(quantized_inputs, x_full):
    owned_rows = quantized_inputs.shape[0]
    wide_count = lax.axis_size("wide")
    columns = owned_rows * lax.axis_size("narrow")
    order = ring_order(wide_count)
    forward = [(order[i], order[(i + 1) % wide_count]) for i in range(wide_count)]
    pairs = (forward, [(b, a) for a, b in forward])
    place = [order.index(w) for w in range(wide_count)]
    me = jnp.asarray(place, jnp.int32)[lax.axis_index("wide")]

    def owner_of(way, distance):
        offset = distance if way == 1 else -distance
        return jnp.asarray(order, jnp.int32)[(me + offset + wide_count) % wide_count]

    out_shape = (wide_count, 1, owned_rows, columns)
    outs = [None, None]
    now = []

    def tie(value, *others):
        held = [i for i in range(2) if outs[i] is not None]
        done = lax.optimization_barrier((value, *[outs[i] for i in held], *now, *others))
        for place_of, i in enumerate(held):
            outs[i] = done[1 + place_of]
        return done[0]

    def put(which, owner, block, out_row=0):
        outs[which] = product(
            tie(block),
            right_own,
            owner=owner,
            out=outs[which],
            out_shape=out_shape,
            out_row=out_row,
        )

    def put_arrived(which, owner, block, first_row):
        outs[which] = lax.dynamic_update_slice(
            outs[which], tie(block).astype(jnp.float32)[None, None], (owner, 0, first_row, 0)
        )

    def gather(block, *others):
        return lax.all_gather(tie(block, *others), "narrow", axis=0, tiled=True)

    q = quantized_inputs
    d = (x_full.astype(jnp.float32) - q.astype(jnp.float32)).astype(jnp.bfloat16)
    right_own = gather(q)

    far, near = wide_count // 2, (wide_count - 1) // 2
    reach = {(0, 0): far, (0, 1): near, (1, 0): near, (1, 1): far}
    raw = {chain: max(hops - 1, min(hops, 1)) for chain, hops in reach.items()}
    at = {(which, way): [[(q, d)[which]]] for which in range(2) for way in range(2)}
    small = owned_rows // QUARTERS
    big = owned_rows - small

    def start(which, step):
        for way in range(2):
            chain = (which, way)
            if step <= raw[chain]:
                parts = at[chain][step - 1]
                if chain == (1, 1) and step == raw[chain] - 1:
                    parts = [parts[0][:big], parts[0][big:]]
                if step > 1:
                    now[:] = at[chain][step - 1][:1]
                    parts = [tie(part) for part in parts]
                at[chain].append([lax.ppermute(part, "wide", pairs[way]) for part in parts])

    def arrivals(which, step):
        return [at[which, way][step][0] for way in range(2) if step <= raw[which, way]]

    def send(which, way, step, block, rows, row=0, out_row=0):
        result = product(tie(block), right_next[way], rows=rows, row=row)
        now.append(result)
        moved = lax.ppermute(result, "wide", pairs[way])
        results.append((which, owner_of(way, step + 1), moved, out_row))

    def is_last(which, way, step):
        return step == raw[which, way] < reach[which, way]

    start(0, 1)
    start(1, 1)
    right_next = [None, None]
    results = []
    for step in range(1, far + 1):
        for which in range(2):
            if not arrivals(which, step):
                continue
            start(which, step + 1)
            now[:] = arrivals(which, step)
            if step == 1 and which == 0:
                for way in range(2):
                    if raw[0, 1 - way] >= 1:
                        right_next[way] = gather(at[0, 1 - way][1][0], d)
            together = step in (1, far - 1)
            if which == 0 and together:
                continue
            if which == 1:
                for chain in ((1, 0), (0, 1)):
                    if is_last(*chain, step):
                        send(*chain, step, at[chain][step][0], owned_rows)
                for chain in ((0, 0), (1, 1)):
                    if is_last(*chain, step):
                        send(*chain, step, at[chain][step][0], big)
            if step == 1:
                put(0, lax.axis_index("wide"), q)
                put(1, lax.axis_index("wide"), d)
            for own in range(2) if together else (which,):
                for way in range(2):
                    if step <= raw[own, way]:
                        put(own, owner_of(way, step), at[own, way][step][0])
            if which == 1:
                for chain in ((1, 1), (0, 0)):
                    if is_last(*chain, step):
                        parts = at[chain][step]
                        row = 0 if len(parts) == 2 else big
                        if chain == (0, 0) and len(results) > 4:
                            put_arrived(*results.pop(0))
                        send(*chain, step, parts[-1], small, row, big)
                for way in range(2):
                    if step <= raw[1, way] and len(at[1, way][step]) == 2:
                        put(1, owner_of(way, step), at[1, way][step][1], big)
    now[:] = []
    for result in sorted(results, key=lambda result: result[3]):
        put_arrived(*result)
    return tuple(outs)


def solution(mesh):
    return jax.shard_map(
        per_device,
        mesh=mesh,
        in_specs=(P(("wide", "narrow"), None), P(("wide", "narrow"), None)),
        out_specs=(P(None, "narrow", None, "wide"), P(None, "narrow", None, "wide")),
        check_vma=False,
    )
```

```python
import functools

import jax
import jax.numpy as jnp
from jax import lax
from jax.experimental import pallas as pl
from jax.experimental.pallas import tpu as pltpu
from jax.sharding import PartitionSpec as P

TILE = 512
QUARTERS = 4


def product_kernel(scale, place_ref, left_ref, right_ref, *refs):
    total = lax.dot_general(
        left_ref[...],
        right_ref[...],
        (((1,), (1,)), ((), ())),
        preferred_element_type=jnp.float32,
    )
    result_ref = refs[-1]
    result_ref[...] = (total * scale).astype(result_ref.dtype).reshape(result_ref.shape)


def product(left, right, owner=None, out=None, out_shape=None, first_row=0, rows=None):
    rows, tokens = rows or left.shape[0], left.shape[1]
    columns = right.shape[0]
    tile = min(TILE, columns)
    if owner is None:
        owner = 0
        out_spec = pl.BlockSpec((rows, tile), lambda j, at: (0, j))
        shape = jax.ShapeDtypeStruct((rows, columns), jnp.bfloat16)
    else:
        out_spec = pl.BlockSpec((1, 1, rows, tile), lambda j, at: (at[0], 0, 0, j))
        shape = jax.ShapeDtypeStruct(out_shape, jnp.float32)
    in_specs = [
        pl.BlockSpec((rows, tokens), lambda j, at: (first_row // rows, 0)),
        pl.BlockSpec((tile, tokens), lambda j, at: (j, 0)),
    ]
    operands = [jnp.asarray(owner, jnp.int32).reshape(1), left, right]
    aliases = {}
    if out is not None:
        aliases = {len(operands): 0}
        in_specs.append(pl.BlockSpec(memory_space=pl.ANY))
        operands.append(out)
    return pl.pallas_call(
        functools.partial(product_kernel, 1.0 / tokens),
        out_shape=shape,
        grid_spec=pltpu.PrefetchScalarGridSpec(
            num_scalar_prefetch=1,
            grid=(columns // tile,),
            in_specs=in_specs,
            out_specs=out_spec,
        ),
        input_output_aliases=aliases,
        compiler_params=pltpu.CompilerParams(vmem_limit_bytes=32 * 1024 * 1024),
        cost_estimate=pl.CostEstimate(flops=0, bytes_accessed=0, transcendentals=0),
    )(*operands)


def ring_order(count):
    return [i for i in range(0, count, 2)] + [i for i in reversed(range(1, count, 2))]


def per_device(quantized_inputs, x_full):
    owned_rows = quantized_inputs.shape[0]
    wide_count = lax.axis_size("wide")
    columns = owned_rows * lax.axis_size("narrow")
    order = ring_order(wide_count)
    forward = [(order[i], order[(i + 1) % wide_count]) for i in range(wide_count)]
    pairs = (forward, [(b, a) for a, b in forward])
    place = [order.index(w) for w in range(wide_count)]
    me = jnp.asarray(place, jnp.int32)[lax.axis_index("wide")]

    def owner_of(way, distance):
        offset = distance if way == 1 else -distance
        return jnp.asarray(order, jnp.int32)[(me + offset + wide_count) % wide_count]

    out_shape = (wide_count, 1, owned_rows, columns)
    outs = [None, None]
    now = []

    def tie(value, *others):
        held = [i for i in range(2) if outs[i] is not None]
        done = lax.optimization_barrier((value, *[outs[i] for i in held], *now, *others))
        for place_of, i in enumerate(held):
            outs[i] = done[1 + place_of]
        return done[0]

    def put(which, owner, block):
        outs[which] = product(tie(block), right_own, owner, outs[which], out_shape)

    def put_arrived(which, owner, block, first_row):
        outs[which] = lax.dynamic_update_slice(
            outs[which], tie(block).astype(jnp.float32)[None, None], (owner, 0, first_row, 0)
        )

    def gather(block, *others):
        return lax.all_gather(tie(block, *others), "narrow", axis=0, tiled=True)

    q = quantized_inputs
    d = (x_full.astype(jnp.float32) - q.astype(jnp.float32)).astype(jnp.bfloat16)
    right_own = gather(q)

    far, near = wide_count // 2, (wide_count - 1) // 2
    reach = {(0, 0): far, (0, 1): near, (1, 0): near, (1, 1): far}
    raw = {chain: max(hops - 1, min(hops, 1)) for chain, hops in reach.items()}
    at = {(which, way): [(q, d)[which]] for which in range(2) for way in range(2)}

    def start(chain, step):
        if step <= raw[chain]:
            block = at[chain][step - 1]
            block = block if step == 1 else tie(block)
            at[chain].append(lax.ppermute(block, "wide", pairs[chain[1]]))

    def send(chain, step, first_row, rows):
        which, way = chain
        result = product(tie(at[chain][step]), right_next[way], first_row=first_row, rows=rows)
        now.append(result)
        moved = lax.ppermute(result, "wide", pairs[way])
        results.append((which, owner_of(way, step + 1), moved, first_row))

    def is_last(chain, step):
        return step == raw[chain] < reach[chain]

    far_chains, near_chains = ((0, 0), (1, 1)), ((1, 0), (0, 1))
    for chain in ((0, 0), (0, 1), (1, 1), (1, 0)):
        start(chain, 1)
    right_next = [None, None]
    results = []
    for step in range(1, far + 1):
        for chains in (far_chains, near_chains):
            here = [chain for chain in chains if step <= raw[chain]]
            if not here:
                continue
            now[:] = [at[chain][step] for chain in (raw if step == 1 else here) if step <= raw[chain]]
            if step == 1 and chains == far_chains and near > 0:
                moved = lax.optimization_barrier((at[0, 0][1], at[0, 1][1]))
                moved = lax.optimization_barrier((*moved, at[1, 0][1], at[1, 1][1]))
                for way in range(2):
                    right_next[way] = gather(moved[1 - way])
            for chain in chains:
                start(chain, step + 1)
            cut = owned_rows - owned_rows // QUARTERS if step == far - 1 else owned_rows
            late = [chain for chain in here if is_last(chain, step) and step < far - 1 and chain[1]]
            for chain in here:
                if is_last(chain, step) and chain not in late:
                    send(chain, step, 0, cut)
                    if cut < owned_rows:
                        send(chain, step, cut, owned_rows - cut)
            if step == 1 and chains == far_chains:
                continue
            if step == 1:
                put(0, lax.axis_index("wide"), q)
                put(1, lax.axis_index("wide"), d)
            for chain in (*far_chains, *near_chains) if step == 1 else here:
                if step <= raw[chain]:
                    put(chain[0], owner_of(chain[1], step), at[chain][step])
            for chain in late:
                send(chain, step, 0, owned_rows)
    now[:] = []
    for result in sorted(results, key=lambda result: result[3]):
        put_arrived(*result)
    return tuple(outs)


def solution(mesh):
    return jax.shard_map(
        per_device,
        mesh=mesh,
        in_specs=(P(("wide", "narrow"), None), P(("wide", "narrow"), None)),
        out_specs=(P(None, "narrow", None, "wide"), P(None, "narrow", None, "wide")),
        check_vma=False,
    )
```

```python
import functools

import jax
import jax.numpy as jnp
from jax import lax
from jax.experimental import pallas as pl
from jax.experimental.pallas import tpu as pltpu
from jax.sharding import PartitionSpec as P

TILE = 512
QUARTERS = 4


def product_kernel(scale, count, place_ref, left_ref, right_ref, *refs):
    results = refs[-count:]
    total = scale * lax.dot_general(
        left_ref[...],
        right_ref[...],
        (((1,), (1,)), ((), ())),
        preferred_element_type=jnp.float32,
    )
    row = 0
    for result_ref in results:
        rows = result_ref.shape[-2]
        part = total[row : row + rows].astype(result_ref.dtype)
        result_ref[...] = part.reshape(result_ref.shape)
        row += rows


def product(left, right, owner=None, out=None, out_shape=None, first_row=0, result_rows=None):
    rows, tokens = sum(result_rows or left.shape[:1]), left.shape[1]
    columns = right.shape[0]
    tile = min(TILE, columns)
    if owner is None:
        owner = 0
        out_specs = [pl.BlockSpec((part, tile), lambda j, at: (0, j)) for part in result_rows]
        shapes = [jax.ShapeDtypeStruct((part, columns), jnp.bfloat16) for part in result_rows]
    else:
        out_specs = [pl.BlockSpec((1, 1, rows, tile), lambda j, at: (at[0], 0, 0, j))]
        shapes = [jax.ShapeDtypeStruct(out_shape, jnp.float32)]
    in_specs = [
        pl.BlockSpec((rows, tokens), lambda j, at: (first_row // rows, 0)),
        pl.BlockSpec((tile, tokens), lambda j, at: (j, 0)),
    ]
    operands = [jnp.asarray(owner, jnp.int32).reshape(1), left, right]
    aliases = {}
    if out is not None:
        aliases = {len(operands): 0}
        in_specs.append(pl.BlockSpec(memory_space=pl.ANY))
        operands.append(out)
    return pl.pallas_call(
        functools.partial(product_kernel, 1.0 / tokens, len(shapes)),
        out_shape=shapes,
        grid_spec=pltpu.PrefetchScalarGridSpec(
            num_scalar_prefetch=1,
            grid=(columns // tile,),
            in_specs=in_specs,
            out_specs=out_specs,
        ),
        input_output_aliases=aliases,
        compiler_params=pltpu.CompilerParams(vmem_limit_bytes=48 * 1024 * 1024),
        cost_estimate=pl.CostEstimate(flops=0, bytes_accessed=0, transcendentals=0),
    )(*operands)


def ring_order(count):
    return [i for i in range(0, count, 2)] + [i for i in reversed(range(1, count, 2))]


def per_device(quantized_inputs, x_full):
    owned_rows = quantized_inputs.shape[0]
    wide_count = lax.axis_size("wide")
    columns = owned_rows * lax.axis_size("narrow")
    order = ring_order(wide_count)
    forward = [(order[i], order[(i + 1) % wide_count]) for i in range(wide_count)]
    pairs = (forward, [(b, a) for a, b in forward])
    place = [order.index(w) for w in range(wide_count)]
    me = jnp.asarray(place, jnp.int32)[lax.axis_index("wide")]

    def owner_of(way, distance):
        offset = distance if way == 1 else -distance
        return jnp.asarray(order, jnp.int32)[(me + offset + wide_count) % wide_count]

    out_shape = (wide_count, 1, owned_rows, columns)
    outs = [None, None]
    now = []

    def tie(value, *others):
        held = [i for i in range(2) if outs[i] is not None]
        done = lax.optimization_barrier((value, *[outs[i] for i in held], *now, *others))
        for place_of, i in enumerate(held):
            outs[i] = done[1 + place_of]
        return done[0]

    def put(which, owner, block):
        (outs[which],) = product(tie(block), right_own, owner, outs[which], out_shape)

    def put_arrived(which, owner, block, first_row):
        outs[which] = lax.dynamic_update_slice(
            outs[which], tie(block).astype(jnp.float32)[None, None], (owner, 0, first_row, 0)
        )

    def gather(block, *others):
        return lax.all_gather(tie(block, *others), "narrow", axis=0, tiled=True)

    q = quantized_inputs
    d = (x_full.astype(jnp.float32) - q.astype(jnp.float32)).astype(jnp.bfloat16)
    right_own = gather(q)

    far, near = wide_count // 2, (wide_count - 1) // 2
    reach = {(0, 0): far, (0, 1): near, (1, 0): near, (1, 1): far}
    raw = {chain: max(hops - 1, min(hops, 1)) for chain, hops in reach.items()}
    at = {(which, way): [(q, d)[which]] for which in range(2) for way in range(2)}

    def start(chain, step):
        if step <= raw[chain]:
            block = at[chain][step - 1]
            block = block if step == 1 else tie(block)
            at[chain].append(lax.ppermute(block, "wide", pairs[chain[1]]))

    def send(chain, step, result_rows, row=0):
        which, way = chain
        parts = product(
            tie(at[chain][step]), right_next[way], first_row=row, result_rows=result_rows
        )
        now.extend(parts)
        for part in parts:
            moved = lax.ppermute(part, "wide", pairs[way])
            results.append((which, owner_of(way, step + 1), moved, row))
            row += part.shape[0]

    def is_last(chain, step):
        return step == raw[chain] < reach[chain]

    far_chains, near_chains = ((0, 0), (1, 1)), ((1, 0), (0, 1))
    for chain in ((0, 0), (0, 1), (1, 1), (1, 0)):
        start(chain, 1)
    right_next = [None, None]
    results = []
    for step in range(1, far + 1):
        for chains in (far_chains, near_chains):
            here = [chain for chain in chains if step <= raw[chain]]
            if not here:
                continue
            now[:] = [at[chain][step] for chain in (raw if step == 1 else here) if step <= raw[chain]]
            if step == 1 and chains == far_chains and near > 0:
                moved = lax.optimization_barrier((at[0, 0][1], at[0, 1][1]))
                moved = lax.optimization_barrier((*moved, at[1, 0][1], at[1, 1][1]))
                for way in range(2):
                    right_next[way] = gather(moved[1 - way])
            for chain in chains:
                start(chain, step + 1)
            late = [chain for chain in here if is_last(chain, step) and step < far - 1 and chain[1]]
            for chain in here:
                if is_last(chain, step) and chain not in late:
                    last = owned_rows // QUARTERS if step == far - 1 else 0
                    if not last:
                        send(chain, step, [owned_rows])
                    elif chain[1] == 0:
                        send(chain, step, [owned_rows - last, last])
                    else:
                        send(chain, step, [owned_rows - last])
                        send(chain, step, [last], owned_rows - last)
            if step == 1 and chains == far_chains:
                continue
            if step == 1:
                put(0, lax.axis_index("wide"), q)
                put(1, lax.axis_index("wide"), d)
            for chain in (*far_chains, *near_chains) if step == 1 else here:
                if step <= raw[chain]:
                    put(chain[0], owner_of(chain[1], step), at[chain][step])
            for chain in late:
                send(chain, step, [owned_rows])
    now[:] = []
    for result in sorted(results, key=lambda result: result[3]):
        put_arrived(*result)
    return tuple(outs)


def solution(mesh):
    return jax.shard_map(
        per_device,
        mesh=mesh,
        in_specs=(P(("wide", "narrow"), None), P(("wide", "narrow"), None)),
        out_specs=(P(None, "narrow", None, "wide"), P(None, "narrow", None, "wide")),
        check_vma=False,
    )
```

```python
import functools

import jax
import jax.numpy as jnp
from jax import lax
from jax.experimental import pallas as pl
from jax.experimental.pallas import tpu as pltpu
from jax.sharding import PartitionSpec as P

TILE = 512
QUARTERS = 4


def product_kernel(scale, count, place_ref, left_ref, right_ref, *refs):
    results = refs[-count:]
    total = scale * lax.dot_general(
        left_ref[...],
        right_ref[...],
        (((1,), (1,)), ((), ())),
        preferred_element_type=jnp.float32,
    )
    row = 0
    for result_ref in results:
        rows = result_ref.shape[-2]
        part = total[row : row + rows].astype(result_ref.dtype)
        result_ref[...] = part.reshape(result_ref.shape)
        row += rows


def product(left, right, owner=None, out=None, out_shape=None, first_row=0, result_rows=None):
    rows, tokens = sum(result_rows or left.shape[:1]), left.shape[1]
    columns = right.shape[0]
    tile = min(TILE, columns)
    if owner is None:
        owner = 0
        out_specs = [pl.BlockSpec((part, tile), lambda j, at: (0, j)) for part in result_rows]
        shapes = [jax.ShapeDtypeStruct((part, columns), jnp.bfloat16) for part in result_rows]
    else:
        out_specs = [pl.BlockSpec((1, 1, rows, tile), lambda j, at: (at[0], 0, 0, j))]
        shapes = [jax.ShapeDtypeStruct(out_shape, jnp.float32)]
    in_specs = [
        pl.BlockSpec((rows, tokens), lambda j, at: (first_row // rows, 0)),
        pl.BlockSpec((tile, tokens), lambda j, at: (j, 0)),
    ]
    operands = [jnp.asarray(owner, jnp.int32).reshape(1), left, right]
    aliases = {}
    if out is not None:
        aliases = {len(operands): 0}
        in_specs.append(pl.BlockSpec(memory_space=pl.ANY))
        operands.append(out)
    return pl.pallas_call(
        functools.partial(product_kernel, 1.0 / tokens, len(shapes)),
        out_shape=shapes,
        grid_spec=pltpu.PrefetchScalarGridSpec(
            num_scalar_prefetch=1,
            grid=(columns // tile,),
            in_specs=in_specs,
            out_specs=out_specs,
        ),
        input_output_aliases=aliases,
        compiler_params=pltpu.CompilerParams(vmem_limit_bytes=32 * 1024 * 1024),
        cost_estimate=pl.CostEstimate(
            flops=4 * rows * columns * tokens if result_rows is None else 0,
            bytes_accessed=0,
            transcendentals=0,
        ),
    )(*operands)


def ring_order(count):
    return [i for i in range(0, count, 2)] + [i for i in reversed(range(1, count, 2))]


def per_device(quantized_inputs, x_full):
    owned_rows = quantized_inputs.shape[0]
    wide_count = lax.axis_size("wide")
    columns = owned_rows * lax.axis_size("narrow")
    order = ring_order(wide_count)
    forward = [(order[i], order[(i + 1) % wide_count]) for i in range(wide_count)]
    pairs = (forward, [(b, a) for a, b in forward])
    place = [order.index(w) for w in range(wide_count)]
    me = jnp.asarray(place, jnp.int32)[lax.axis_index("wide")]

    def owner_of(way, distance):
        offset = distance if way == 1 else -distance
        return jnp.asarray(order, jnp.int32)[(me + offset + wide_count) % wide_count]

    out_shape = (wide_count, 1, owned_rows, columns)
    outs = [None, None]
    now = []

    def tie(value, *others):
        held = [i for i in range(2) if outs[i] is not None]
        done = lax.optimization_barrier((value, *[outs[i] for i in held], *now, *others))
        for place_of, i in enumerate(held):
            outs[i] = done[1 + place_of]
        return done[0]

    def put(which, owner, block):
        (outs[which],) = product(tie(block), right_own, owner, outs[which], out_shape)

    def put_arrived(which, owner, block, first_row):
        outs[which] = lax.dynamic_update_slice(
            outs[which], tie(block).astype(jnp.float32)[None, None], (owner, 0, first_row, 0)
        )

    def gather(block, *others):
        return lax.all_gather(tie(block, *others), "narrow", axis=0, tiled=True)

    q = quantized_inputs
    d = (x_full.astype(jnp.float32) - q.astype(jnp.float32)).astype(jnp.bfloat16)
    right_own = gather(q)

    far, near = wide_count // 2, (wide_count - 1) // 2
    reach = {(0, 0): far, (0, 1): near, (1, 0): near, (1, 1): far}
    raw = {chain: max(hops - 1, min(hops, 1)) for chain, hops in reach.items()}
    at = {(which, way): [(q, d)[which]] for which in range(2) for way in range(2)}

    def start(chain, step):
        if step <= raw[chain]:
            block = at[chain][step - 1]
            block = block if step == 1 else tie(block)
            at[chain].append(lax.ppermute(block, "wide", pairs[chain[1]]))

    def send(chain, step, result_rows, row=0):
        which, way = chain
        parts = product(
            tie(at[chain][step]), right_next[way], first_row=row, result_rows=result_rows
        )
        now.extend(parts)
        for part in parts:
            moved = lax.ppermute(part, "wide", pairs[way])
            results.append((which, owner_of(way, step + 1), moved, row))
            row += part.shape[0]

    def is_last(chain, step):
        return step == raw[chain] < reach[chain]

    far_chains, near_chains = ((0, 0), (1, 1)), ((1, 0), (0, 1))
    for chain in ((0, 0), (0, 1), (1, 1), (1, 0)):
        start(chain, 1)
    right_next = [None, None]
    results, earlier = [], []
    for step in range(1, far + 1):
        for chains in (far_chains, near_chains):
            here = [chain for chain in chains if step <= raw[chain]]
            if not here:
                continue
            now[:] = [at[chain][step] for chain in (raw if step == 1 else here) if step <= raw[chain]]
            now += earlier
            if step == 1 and chains == far_chains and near > 0:
                moved = lax.optimization_barrier((at[0, 0][1], at[0, 1][1]))
                moved = lax.optimization_barrier((*moved, at[1, 0][1], at[1, 1][1]))
                for way in range(2):
                    right_next[way] = gather(moved[1 - way])
            for chain in chains:
                start(chain, step + 1)
            late = [chain for chain in here if is_last(chain, step) and step < far - 1 and chain[1]]
            for chain in here:
                if is_last(chain, step) and chain not in late:
                    last = owned_rows // QUARTERS if step == far - 1 else 0
                    if not last:
                        send(chain, step, [owned_rows])
                    elif chain[1] == 0:
                        send(chain, step, [owned_rows - last, last])
                    else:
                        send(chain, step, [owned_rows - last])
                        send(chain, step, [last], owned_rows - last)
            if step == 1 and chains == far_chains:
                continue
            if step == 1:
                put(0, lax.axis_index("wide"), q)
                put(1, lax.axis_index("wide"), d)
            for chain in (*far_chains, *near_chains) if step == 1 else here:
                if step <= raw[chain]:
                    put(chain[0], owner_of(chain[1], step), at[chain][step])
            for chain in late:
                send(chain, step, [owned_rows])
                earlier.append(now[-1])
    now[:] = []
    for result in sorted(results, key=lambda result: result[3]):
        put_arrived(*result)
    return tuple(outs)


def solution(mesh):
    return jax.shard_map(
        per_device,
        mesh=mesh,
        in_specs=(P(("wide", "narrow"), None), P(("wide", "narrow"), None)),
        out_specs=(P(None, "narrow", None, "wide"), P(None, "narrow", None, "wide")),
        check_vma=False,
    )
```

```python
import functools

import jax
import jax.numpy as jnp
from jax import lax
from jax.experimental import pallas as pl
from jax.experimental.pallas import tpu as pltpu
from jax.sharding import PartitionSpec as P

TILE = 512
QUARTERS = 4


def product_kernel(scale, count, place_ref, left_ref, right_ref, *refs):
    results = refs[-count:]
    total = scale * lax.dot_general(
        left_ref[...],
        right_ref[...],
        (((1,), (1,)), ((), ())),
        preferred_element_type=jnp.float32,
    )
    row = 0
    for result_ref in results:
        rows = result_ref.shape[-2]
        part = total[row : row + rows].astype(result_ref.dtype)
        result_ref[...] = part.reshape(result_ref.shape)
        row += rows


def product(left, right, owner=None, out=None, out_shape=None, first_row=0, result_rows=None):
    rows, tokens = sum(result_rows or left.shape[:1]), left.shape[1]
    columns = right.shape[0]
    tile = min(TILE, columns)
    if owner is None:
        owner = 0
        out_specs = [pl.BlockSpec((part, tile), lambda j, at: (0, j)) for part in result_rows]
        shapes = [jax.ShapeDtypeStruct((part, columns), jnp.bfloat16) for part in result_rows]
    else:
        out_specs = [pl.BlockSpec((1, 1, rows, tile), lambda j, at: (at[0], 0, 0, j))]
        shapes = [jax.ShapeDtypeStruct(out_shape, jnp.float32)]
    in_specs = [
        pl.BlockSpec((rows, tokens), lambda j, at: (first_row // rows, 0)),
        pl.BlockSpec((tile, tokens), lambda j, at: (j, 0)),
    ]
    operands = [jnp.asarray(owner, jnp.int32).reshape(1), left, right]
    aliases = {}
    if out is not None:
        aliases = {len(operands): 0}
        in_specs.append(pl.BlockSpec(memory_space=pl.ANY))
        operands.append(out)
    return pl.pallas_call(
        functools.partial(product_kernel, 1.0 / tokens, len(shapes)),
        out_shape=shapes,
        grid_spec=pltpu.PrefetchScalarGridSpec(
            num_scalar_prefetch=1,
            grid=(columns // tile,),
            in_specs=in_specs,
            out_specs=out_specs,
        ),
        input_output_aliases=aliases,
        compiler_params=pltpu.CompilerParams(vmem_limit_bytes=32 * 1024 * 1024),
        cost_estimate=pl.CostEstimate(flops=0, bytes_accessed=0, transcendentals=0),
    )(*operands)


def ring_order(count):
    return [i for i in range(0, count, 2)] + [i for i in reversed(range(1, count, 2))]


def per_device(quantized_inputs, x_full):
    owned_rows = quantized_inputs.shape[0]
    wide_count = lax.axis_size("wide")
    columns = owned_rows * lax.axis_size("narrow")
    order = ring_order(wide_count)
    forward = [(order[i], order[(i + 1) % wide_count]) for i in range(wide_count)]
    pairs = (forward, [(b, a) for a, b in forward])
    place = [order.index(w) for w in range(wide_count)]
    me = jnp.asarray(place, jnp.int32)[lax.axis_index("wide")]

    def owner_of(way, distance):
        offset = distance if way == 1 else -distance
        return jnp.asarray(order, jnp.int32)[(me + offset + wide_count) % wide_count]

    out_shape = (wide_count, 1, owned_rows, columns)
    outs = [None, None]
    now = []

    def tie(value, *others):
        held = [i for i in range(2) if outs[i] is not None]
        done = lax.optimization_barrier((value, *[outs[i] for i in held], *now, *others))
        for place_of, i in enumerate(held):
            outs[i] = done[1 + place_of]
        return done[0]

    def put(which, owner, block):
        (outs[which],) = product(tie(block), right_own, owner, outs[which], out_shape)

    def put_arrived(which, owner, block, first_row):
        outs[which] = lax.dynamic_update_slice(
            outs[which], tie(block).astype(jnp.float32)[None, None], (owner, 0, first_row, 0)
        )

    def gather(block, *others):
        return lax.all_gather(tie(block, *others), "narrow", axis=0, tiled=True)

    q = quantized_inputs
    d = (x_full.astype(jnp.float32) - q.astype(jnp.float32)).astype(jnp.bfloat16)
    right_own = gather(q)

    far, near = wide_count // 2, (wide_count - 1) // 2
    reach = {(0, 0): far, (0, 1): near, (1, 0): near, (1, 1): far}
    raw = {chain: max(hops - 1, min(hops, 1)) for chain, hops in reach.items()}
    at = {(which, way): [(q, d)[which]] for which in range(2) for way in range(2)}

    def start(chain, step):
        if step <= raw[chain]:
            block = at[chain][step - 1]
            block = block if step == 1 else tie(block)
            at[chain].append(lax.ppermute(block, "wide", pairs[chain[1]]))

    def send(chain, step, result_rows, row=0):
        which, way = chain
        parts = product(
            tie(at[chain][step]), right_next[way], first_row=row, result_rows=result_rows
        )
        now.extend(parts)
        for part in parts:
            moved = lax.ppermute(part, "wide", pairs[way])
            results.append((which, owner_of(way, step + 1), moved, row))
            row += part.shape[0]

    def is_last(chain, step):
        return step == raw[chain] < reach[chain]

    far_chains, near_chains = ((0, 0), (1, 1)), ((1, 0), (0, 1))
    for chain in ((0, 0), (0, 1), (1, 1), (1, 0)):
        start(chain, 1)
    right_next = [None, None]
    results = []
    for step in range(1, far + 1):
        for chains in (far_chains, near_chains):
            here = [chain for chain in chains if step <= raw[chain]]
            if not here:
                continue
            now[:] = [at[chain][step] for chain in (raw if step == 1 else here) if step <= raw[chain]]
            if step == 1 and chains == far_chains and near > 0:
                moved = lax.optimization_barrier((at[0, 0][1], at[0, 1][1]))
                moved = lax.optimization_barrier((*moved, at[1, 0][1], at[1, 1][1]))
                for way in range(2):
                    right_next[way] = gather(moved[1 - way])
            for chain in chains:
                start(chain, step + 1)
            late = [chain for chain in here if is_last(chain, step) and step < far - 1 and chain[1]]
            for chain in here:
                if is_last(chain, step) and chain not in late:
                    last = owned_rows // QUARTERS if step == far - 1 else 0
                    if not last:
                        send(chain, step, [owned_rows])
                    elif chain[1] == 0:
                        send(chain, step, [owned_rows - last, last])
                    else:
                        send(chain, step, [owned_rows - last])
                        send(chain, step, [last], owned_rows - last)
            if step == 1 and chains == far_chains:
                continue
            if step == 1:
                put(0, lax.axis_index("wide"), q)
                put(1, lax.axis_index("wide"), d)
            for chain in (*far_chains, *near_chains) if step == 1 else here:
                if step <= raw[chain]:
                    put(chain[0], owner_of(chain[1], step), at[chain][step])
            for chain in late:
                send(chain, step, [owned_rows])
    now[:] = []
    for result in sorted(results, key=lambda result: result[3]):
        put_arrived(*result)
    return tuple(outs)


def solution(mesh):
    return jax.shard_map(
        per_device,
        mesh=mesh,
        in_specs=(P(("wide", "narrow"), None), P(("wide", "narrow"), None)),
        out_specs=(P(None, "narrow", None, "wide"), P(None, "narrow", None, "wide")),
        check_vma=False,
    )
```
